32 devices in a mesh: grp: 2 (over x), row: 8 (over z, y), col: 2 (over core).
Axes of the slice: x: 2, y: 2, z: 4, core: 2. Of those that a mesh axis runs over, the one named last changes fastest.
Arguments:
- green: float32 [4, 256, 256, 256], P('grp', None, 'row', 'col'), parts along dimension 0, may hold values from -6 to 6
- hamiltonian: float32 [4, 256, 256], P('grp'), parts along dimension 0
- onebody: float32 [4, 256, 256], P('grp'), parts along dimension 0, may hold values from -5 to 5
- site_map: int32 [256], replicated, may hold values from 0 to 31
- onsite_u: float32 [32], replicated, may hold values from 0.5 to 2
- pair_first: int32 [4096], replicated, may hold values from 0 to 255
- pair_second: int32 [4096], replicated, may hold values from 0 to 255
Outputs:
- advanced: float32 [4, 256, 256, 256], P('grp', None, 'row', 'col'), parts along dimension 0
The draws below stay inside these ranges and needn't reach their ends.
There are 2 independent parts, one for each index of `grp`. The reference program is written for one: setup_inputs(seed, part) draws one part's arguments, and reference() takes and returns one part's arrays. A program takes and returns all parts, laid end to end along the dimension named above; an argument that names none is the same for every part. Nothing has to cross between parts.
All inputs are finite; a program needn't handle non-finite values.
Results may differ from the reference program's by a relative error of at most 0.00005.
Values sent between devices are 32-bit elements; how exact they have to be, the bound alone decides.
A program may use at most 192 MiB of HBM per device.

```python
import math
import jax
import jax.numpy as jnp
from jax import lax

ORB = 256
NSITE = 32
NPAIR = 4096


def draw_hamiltonian(key, part):
    raw = jax.random.normal(key, (2, ORB, ORB), jnp.float32)
    scale = (2.0 * ORB) ** (-0.5)
    real_part = (raw[0] + raw[0].T) * scale
    imag_part = (raw[1] - raw[1].T) * scale
    return jnp.stack([real_part, imag_part]).astype(jnp.float32)


def set_ends(entries, rng, least, largest):
    longest = entries.shape.index(max(entries.shape))
    spots = []
    for shift in (0, 1):
        where = [jax.random.randint(jax.random.fold_in(rng, axis), (), 0, length) for axis, length in enumerate(entries.shape)]
        where[longest] = (where[longest] + shift) % entries.shape[longest]
        spots.append(tuple(where))
    return entries.at[spots[0]].set(least).at[spots[1]].set(largest)


def steps_of(own_key, extent, cuts, least, high):
    factor_of, own = 1.0, jax.random.fold_in(own_key, 6)
    for position, parts in cuts:
        steps = jnp.exp(jax.random.uniform(jax.random.fold_in(own, position), (parts,), jnp.float32, least / len(cuts), high / len(cuts)))
        factor_of = factor_of * jnp.repeat(steps, extent[position] // parts).reshape([-1 if axis == position else 1 for axis in range(len(extent))])
    return factor_of


def noise(stream_key, extent, deviation, bound, shards=(), kind=jnp.bfloat16):
    drawn = deviation * jax.random.normal(stream_key, extent, jnp.float32)
    if shards:
        drawn = drawn * steps_of(stream_key, extent, shards, -0.22, 0.18)
    return jnp.clip(drawn, -bound, bound).astype(kind)


def setup_inputs(seed: int = 0, part: int = 0) -> dict:
    keys = jax.random.split(jax.random.key(seed), 8)
    part_keys = jax.random.split(jax.random.fold_in(keys[7], part), 8)
    green = noise(part_keys[0], (2, ORB, ORB, ORB), 1.0, 6.0, ((2, 8), (3, 2)), jnp.float32)
    hamiltonian = draw_hamiltonian(jax.random.fold_in(jax.random.fold_in(keys[7], part), 71), part)
    onebody = noise(part_keys[2], (2, ORB, ORB), 0.8, 5.0, (), jnp.float32)
    site_map = set_ends(jax.random.randint(keys[3], (ORB,), 0, NSITE), jax.random.fold_in(keys[3], 1), 0, NSITE - 1).astype(jnp.int32)
    onsite_u = jnp.clip(jnp.exp(jax.random.uniform(keys[4], (NSITE,), jnp.float32, math.log(0.5), math.log(2.0))), 0.5, 2.0)
    pair_first = set_ends(jax.random.randint(keys[5], (NPAIR,), 0, ORB), jax.random.fold_in(keys[5], 1), 0, ORB - 1).astype(jnp.int32)
    pair_second = set_ends(jax.random.randint(keys[6], (NPAIR,), 0, ORB), jax.random.fold_in(keys[6], 1), 0, ORB - 1).astype(jnp.int32)
    return {"green": green, "hamiltonian": hamiltonian, "onebody": onebody, "site_map": site_map, "onsite_u": onsite_u, "pair_first": pair_first, "pair_second": pair_second}


time_step = 0.1
highest = lax.Precision.HIGHEST


def complex_terms(hamiltonian, field):
    orbs = field.shape[1]
    hre = hamiltonian[0]
    him = hamiltonian[1]
    flat_re = field[0].reshape(orbs, -1)
    flat_im = field[1].reshape(orbs, -1)
    k_re = jnp.dot(hre, flat_re, precision=highest) - jnp.dot(him, flat_im, precision=highest)
    k_im = jnp.dot(hre, flat_im, precision=highest) + jnp.dot(him, flat_re, precision=highest)
    k_re = k_re.reshape(field[0].shape)
    k_im = k_im.reshape(field[0].shape)
    i_re = jnp.einsum("ia,kaj->kij", hre, field[0], precision=highest) - jnp.einsum("ia,kaj->kij", him, field[1], precision=highest)
    i_im = jnp.einsum("ia,kaj->kij", hre, field[1], precision=highest) + jnp.einsum("ia,kaj->kij", him, field[0], precision=highest)
    j_re = jnp.einsum("ja,kia->kij", hre, field[0], precision=highest) - jnp.einsum("ja,kia->kij", him, field[1], precision=highest)
    j_im = jnp.einsum("ja,kia->kij", hre, field[1], precision=highest) + jnp.einsum("ja,kia->kij", him, field[0], precision=highest)
    return k_re + i_re + j_re, k_im + i_im + j_im


def reference(green, hamiltonian, onebody, site_map, onsite_u, pair_first, pair_second):
    orbs = green.shape[1]
    u_rows = onsite_u[site_map]
    ladder = u_rows[:, None] * (site_map[:, None] == site_map[None, :]).astype(jnp.float32)
    levels = jnp.arange(orbs, dtype=jnp.int32)
    first_hot = (pair_first[:, None] == levels[None, :]).astype(jnp.float32)
    second_hot = (pair_second[:, None] == levels[None, :]).astype(jnp.float32)
    counts = jnp.einsum("pi,pj->ij", first_hot, second_hot, precision=highest)
    pauli = u_rows[:, None] * counts
    left = onebody
    source_re = pauli * (left[0][:, :, None] * left[0][:, None, :] - left[1][:, :, None] * left[1][:, None, :])
    source_im = pauli * (left[0][:, :, None] * left[1][:, None, :] + left[1][:, :, None] * left[0][:, None, :])

    def force(field):
        hop_re, hop_im = complex_terms(hamiltonian, field)
        total_re = hop_re + ladder * field[0] + source_re
        total_im = hop_im + ladder * field[1] + source_im
        return jnp.stack([total_im, -total_re])

    half = green + (0.5 * time_step) * force(green)
    return green + time_step * force(half)
```

```python
import functools

import jax
import jax.numpy as jnp
from jax import lax
from jax.experimental import pallas as pl
from jax.experimental.pallas import tpu as pltpu
from jax.sharding import Mesh, PartitionSpec as P

time_step = 0.1
highest = lax.Precision.HIGHEST
high = lax.Precision.HIGH
f32 = jnp.float32
bf16 = jnp.bfloat16


def split(x):
    upper = x.astype(bf16)
    return upper, (x - upper.astype(f32)).astype(bf16)


def stack_right(x):
    upper, lower = split(x)
    return jnp.concatenate([upper, lower, upper], axis=0)


def stack_left(x):
    upper, lower = split(x)
    return jnp.concatenate([upper, lower, upper], axis=1)


def dot(a, b):
    return jnp.dot(a, b, preferred_element_type=f32)


def pair_kernel(ncol, place, own_ref, *refs):
    nown = own_ref.shape[0]
    far_refs = refs[:nown]
    (left_ref, left_own_ref, right_ref, hi_ref, hown_ref, hj_ref, ladder_ref, ladder_own_ref,
     pauli_ref, pauli_own_ref, out_ref, field, hcat, hown, wcat) = refs[nown:]
    orbs = ladder_ref.shape[0]
    half = orbs // 2
    _, _, _, nr, nc = own_ref.shape
    mine, me = place[0], place[1]

    @pl.when(pl.program_id(0) == 0)
    def _():
        upper, lower = split(hi_ref[...])
        hcat[...] = jnp.concatenate([upper, upper, lower], axis=1)
        upper, lower = split(hown_ref[...])
        hown[...] = jnp.concatenate([upper, upper, lower], axis=1)
        upper, lower = split(hj_ref[...])
        wcat[...] = jnp.concatenate([upper, upper, lower], axis=0)

    for n in range(nown):
        r, c = divmod(n, ncol)
        low = pl.multiple_of(mine * half + r * nr, nr)
        source = me ^ n
        far_low = pl.multiple_of((1 - mine) * half + lax.div(source, ncol) * nr, nr)
        far_col = pl.multiple_of(lax.rem(source, ncol) * nc, nc)
        for d in range(2):
            field[pl.ds(d * orbs + low, nr), pl.ds(c * nc, nc)] = own_ref[n, 0, d]
            field[pl.ds(d * orbs + far_low, nr), pl.ds(far_col, nc)] = far_refs[n][0, d]

    def apply(x, matrix, rhs, lhs, ladder):
        size = x.shape[0] // 2
        rows = dot(matrix, rhs)
        cols = dot(lhs, wcat[...])
        re = rows[:size] + (cols[:size, :orbs] - cols[size:, orbs:]) + ladder * x[:size]
        im = rows[size:] + (cols[:size, orbs:] + cols[size:, :orbs]) + ladder * x[size:]
        return re, im

    def source_of(left, pauli):
        lre, lim = left[0, 0], left[0, 1]
        rre, rim = right_ref[0, 0], right_ref[0, 1]
        return pauli * (lre * rre - lim * rim), pauli * (lre * rim + lim * rre)

    x = field[...]
    sre, sim = source_of(left_ref, pauli_ref[...])
    mre, mim = apply(x, hcat[...], stack_right(x), stack_left(x), ladder_ref[...])
    field[pl.ds(0, orbs), :] = mre + sre
    field[pl.ds(orbs, orbs), :] = mim + sim
    low = pl.multiple_of(mine * half, half)
    pre = field[pl.ds(low, half), :]
    pim = field[pl.ds(orbs + low, half), :]
    x = jnp.concatenate([pre, pim], axis=0)
    vre, vim = apply(x, hown[...], stack_right(field[...]), stack_left(x), ladder_own_ref[...])
    sre, sim = source_of(left_own_ref, pauli_own_ref[...])
    qre, qim = pre - 0.5 * sre, pim - 0.5 * sim
    scale = 0.5 * time_step * time_step
    ure = time_step * pim - scale * vre
    uim = -time_step * pre - scale * vim
    for n in range(nown):
        r, c = divmod(n, ncol)
        at = (slice(r * nr, (r + 1) * nr), slice(c * nc, (c + 1) * nc))
        out_ref[n, 0, 0] = qre[at]
        out_ref[n, 0, 1] = qim[at]
        out_ref[n, 0, 2] = ure[at]
        out_ref[n, 0, 3] = uim[at]


def pair_apply(ncol, place, own, far, left, left_own, right, constants):
    nown, nk, _, nr, nc = own.shape
    orbs = right.shape[-1]
    half = orbs // 2
    block = pl.BlockSpec((nown, 1, 2, nr, nc), lambda k, place: (0, k, 0, 0, 0))

    def each(a):
        return pl.BlockSpec((1,) + a.shape[1:], lambda k, place: (k, 0, 0, 0))

    def whole(a):
        return pl.BlockSpec(a.shape, lambda k, place: (0, 0))

    return pl.pallas_call(
        functools.partial(pair_kernel, ncol),
        grid_spec=pltpu.PrefetchScalarGridSpec(
            num_scalar_prefetch=1,
            grid=(nk,),
            in_specs=[block]
            + [each(a) for a in far]
            + [each(left), each(left_own), each(right)]
            + [whole(a) for a in constants],
            out_specs=pl.BlockSpec((nown, 1, 4, nr, nc), lambda k, place: (0, k, 0, 0, 0)),
            scratch_shapes=[
                pltpu.VMEM((2 * orbs, orbs), f32),
                pltpu.VMEM((2 * orbs, 6 * orbs), bf16),
                pltpu.VMEM((2 * half, 6 * orbs), bf16),
                pltpu.VMEM((3 * orbs, 2 * orbs), bf16),
            ],
        ),
        out_shape=jax.ShapeDtypeStruct((nown, nk, 4, nr, nc), f32),
        compiler_params=pltpu.CompilerParams(vmem_limit_bytes=48 * 1024 * 1024),
        cost_estimate=pl.CostEstimate(
            flops=nk * 72 * orbs**3, bytes_accessed=16 * own.size, transcendentals=0
        ),
    )(place, own, *far, left, left_own, right, *constants)


def on_device(nquad, ncol, chunks, green, hamiltonian, onebody, site_map, onsite_u, pair_first, pair_second):
    orbs, nr, nc = green.shape[1:]
    nown = nquad * ncol
    half = orbs // 2
    nk = orbs // (nown * chunks)
    mine = lax.axis_index("half")
    me = lax.axis_index("quad") * ncol + lax.axis_index("col")
    place = jnp.stack([mine, me]).astype(jnp.int32)

    packed = jnp.transpose(green.reshape(2, nown, chunks, nk, nr, nc), (2, 1, 3, 0, 4, 5))

    def exchange(x):
        return lax.all_to_all(x, ("quad", "col"), split_axis=0, concat_axis=0, tiled=True)

    def across(x, m):
        part = lax.dynamic_index_in_dim(x, me ^ m, 0, keepdims=False)
        pairs = [(s * nown + e, (1 - s) * nown + (e ^ m)) for s in range(2) for e in range(nown)]
        return lax.ppermute(part, ("half", "quad", "col"), pairs)

    far = [[across(packed[n], m) for m in range(nown)] for n in range(chunks)]
    own = [exchange(packed[n]) for n in range(chunks)]

    levels = jnp.arange(onsite_u.shape[0], dtype=jnp.int32)
    u_rows = jnp.sum(jnp.where(site_map[:, None] == levels[None, :], onsite_u[None, :], 0.0), axis=1)
    ladder = u_rows[:, None] * (site_map[:, None] == site_map[None, :]).astype(f32)
    orbitals = jnp.arange(orbs, dtype=jnp.int32)
    first_hot = (orbitals[:, None] == pair_first[None, :]).astype(bf16)
    second_hot = (orbitals[:, None] == pair_second[None, :]).astype(bf16)
    counts = jnp.einsum("ip,jp->ij", first_hot, second_hot, preferred_element_type=f32)
    pauli = u_rows[:, None] * counts

    hre, him = hamiltonian[0], hamiltonian[1]
    hi = jnp.concatenate(
        [jnp.concatenate([hre, -him], axis=1), jnp.concatenate([him, hre], axis=1)], axis=0
    )
    hj = jnp.concatenate([hre.T, him.T], axis=1)
    square = jnp.dot(hi, hi, precision=highest)
    spin = jnp.concatenate([hi[orbs:], -hi[:orbs]], axis=0)
    scale = 0.5 * time_step * time_step
    near = (time_step * spin - scale * square).reshape(2, orbs, 2, orbs)
    cross = (-2.0 * scale * hi).reshape(2, orbs, 2, nown, chunks, nk)

    def rows_of(a, axis):
        return lax.dynamic_slice_in_dim(a, mine * half, half, axis)

    hown = rows_of(hi.reshape(2, orbs, 2 * orbs), 1).reshape(2 * half, 2 * orbs)
    constants = (hi, hown, hj, ladder, rows_of(ladder, 0), pauli, rows_of(pauli, 0))
    body = lax.dynamic_slice_in_dim(onebody, me * (chunks * nk), chunks * nk, 1)
    body = jnp.transpose(body.reshape(2, chunks, nk, orbs), (1, 2, 0, 3))
    body_own = rows_of(body, 3)

    fields, ends = [], []
    for n in range(chunks):
        both = pair_apply(
            ncol, place, own[n], far[n], body[n][..., None], body_own[n][..., None],
            body[n][:, :, None, :], constants,
        )
        both = exchange(both)
        fields.append(both[:, :, :2])
        ends.append(both[:, :, 2:])
    total = lax.optimization_barrier(
        green + jnp.einsum("ckdl,dlij->ckij", near, green, precision=high)
    )
    for n in range(chunks):
        total = lax.optimization_barrier(
            total + jnp.einsum("ckdxt,xtdij->ckij", cross[:, :, :, :, n], fields[n], precision=high)
        )
    rest = jnp.stack([jnp.transpose(e, (2, 0, 1, 3, 4)) for e in ends], axis=2)
    return total + rest.reshape(green.shape)


def solution(mesh):
    nrow, ncol = mesh.shape["row"], mesh.shape["col"]
    halves = Mesh(
        mesh.devices.reshape(mesh.shape["grp"], 2, nrow // 2, ncol),
        ("grp", "half", "quad", "col"),
    )
    field = P("grp", None, ("half", "quad"), "col")
    placed = (field, P("grp", None, None), P("grp", None, None), P(), P(), P(), P())
    return jax.shard_map(
        functools.partial(on_device, nrow // 2, ncol, 4),
        mesh=halves,
        in_specs=placed,
        out_specs=field,
        check_vma=False,
    )
```
